32 devices in a mesh: grp: 4 (over x, core), shard: 8 (over z, y).
Axes of the slice: x: 2, y: 2, z: 4, core: 2. Of those that a mesh axis runs over, the one named last changes fastest.
Arguments:
- cand_table: bfloat16 [2048, 512], P('grp'), may hold values from -6 to 6
- inverse: int32 [8192], P(('grp', 'shard')), may hold values from 0 to 2047
- cache_keys: bfloat16 [65536, 512], P(('grp', 'shard')), may hold values from -6 to 6
- cache_values: bfloat16 [65536, 512], P(('grp', 'shard')), may hold values from -6 to 6
- block_dest: int32 [512, 1], P(('grp', 'shard')), may hold values from 0 to 7; in each aligned block of 16 rows (0 to 15, 16 to 31, ...) at most 2 rows name the same one
- w_in: bfloat16 [512, 1024], replicated, may hold values from -0.25 to 0.25
- w_out: bfloat16 [512, 512], replicated, may hold values from -0.25 to 0.25
Outputs:
- scored: bfloat16 [8192, 512], P(('grp', 'shard'))
The draws below stay inside these ranges and needn't reach their ends.
Inputs may be any that keep to these rules, and one draw needn't show every extreme that they name: `block_dest`: among the 16 blocks held by one device, at most 2 name the same scorer.
All inputs are finite; a program needn't handle non-finite values.
Results may differ from the reference program's by a relative error of at most 0.0082.
Values may be sent and summed in bfloat16 or wider, within the bound.
A program may use at most 128 MiB of HBM per device.

```python
import math
import jax
import jax.numpy as jnp
import numpy as np
from jax import lax

D = 512
H = 8
BLK = 128
CB_DEV = 16
MOST = 2
CAND = 256
UNIQ = 2048
CAND_ALL = 8192
BLOCKS = 512
CACHE_ROWS = 65536
N_GRP = 4
N_SHARD = 8


def plant(drawn, rng, least, largest):
    index_at = [jax.random.randint(jax.random.fold_in(rng, axis), (), 0, length) for axis, length in enumerate(drawn.shape)]
    widest = drawn.shape.index(max(drawn.shape))
    neighbour = index_at[:widest] + [(index_at[widest] + 1) % drawn.shape[widest]] + index_at[widest + 1:]
    return drawn.at[tuple(index_at)].set(least).at[tuple(neighbour)].set(largest)


def shard_levels(own_key, dims, shards, low, top_value):
    def one(dim, blocks):
        draws = jax.random.uniform(jax.random.fold_in(jax.random.fold_in(own_key, 6), dim), (blocks,), jnp.float32, low / len(shards), top_value / len(shards))
        return jnp.repeat(jnp.exp(draws), dims[dim] // blocks).reshape((-1,) + (1,) * (len(dims) - dim - 1))

    loudness = one(*shards[0])
    for cut in shards[1:]:
        loudness = loudness * one(*cut)
    return loudness


def deal_out(rng, own, number, rows, count, top, most, slope):
    order = jax.random.permutation(rng, count)
    heavy_load, usual = portions_of(count, rows * top, most, slope, True), portions_of(count, rows * top, most, slope, False)
    places = jnp.arange(count)

    def named(lengths, turn):
        used = int((lengths > 0).sum())
        fixed = max(1, used // 4)
        shifted = fixed + (places - fixed + turn * (used - fixed)) % max(1, count - fixed)
        return jnp.zeros((count,), jnp.int32).at[order[jnp.where(places < fixed, places, shifted)]].set(jnp.asarray(lengths, jnp.int32))

    lengths = jnp.where(number % 4 == 0, named(heavy_load, number // 4), named(usual, number - number // 4 - 1))
    mixed = jax.random.permutation(jax.random.fold_in(own, 3), count)
    giver, sink = mixed[0:count // 2 * 2:2], mixed[1:count // 2 * 2:2]
    slack = jnp.minimum(lengths[giver] - 1, most - lengths[sink]) // 2
    slack = jnp.where((giver == order[0]) | (sink == order[0]) | (lengths[sink] == 0), 0, jnp.maximum(slack, 0))
    shifted = jax.random.randint(jax.random.fold_in(own, 4), (count // 2,), 0, 1 << 20) % (slack + 1)
    lengths = lengths.at[giver].add(-shifted).at[sink].add(shifted)
    labels = jnp.searchsorted(jnp.cumsum(lengths), jnp.arange(rows * top), side="right").astype(jnp.int32)
    grid = labels.reshape(top, rows).T
    grid = grid[jax.random.permutation(jax.random.fold_in(own, 1), rows)]
    turn = jax.random.randint(jax.random.fold_in(own, 2), (rows, 1), 0, top)
    return jnp.take_along_axis(grid, (jnp.arange(top)[None, :] + turn) % top, axis=1)


def portions_of(amount, total, limit, skew, full):
    loads = [(1 << 20) // math.isqrt(standing ** skew) + 1 for standing in range(1, amount + 1)]
    largest = limit if full else min(limit, max(-(-total // amount), total * loads[0] // sum(loads)))
    least = 1 if total - largest >= amount - 1 else 0
    counts, surplus = [largest] + [least] * (amount - 1), total - largest - least * (amount - 1)
    while surplus > 0:
        free = [i for i in range(1, amount) if counts[i] < largest] or [i for i in range(1, amount) if counts[i] < limit]
        mass, budget = sum([loads[i] for i in free]), surplus
        for i in free:
            extra = min(limit - counts[i], max(1, budget * loads[i] // mass), surplus)
            counts[i] = counts[i] + extra
            surplus = surplus - extra
    return np.array(counts)


def gaussian(rng, shape, scale, most, pieces=(), kind=jnp.bfloat16):
    array = jax.random.normal(rng, shape, jnp.float32) * scale
    if len(pieces) > 0:
        array = shard_levels(rng, shape, pieces, -0.22, 0.18) * array
    return jnp.clip(array, min=-most, max=most).astype(kind)


def setup_inputs(seed: int = 0) -> dict:
    arg_keys = jax.random.split(jax.random.key(seed), 8)
    cand_table = gaussian(arg_keys[0], (UNIQ, D), 1.0, 6.0, ((0, 4),))
    inverse = plant(jax.random.randint(arg_keys[1], (CAND_ALL,), 0, UNIQ), jax.random.fold_in(arg_keys[1], 1), 0, UNIQ - 1).astype(jnp.int32)
    cache_keys = gaussian(arg_keys[2], (CACHE_ROWS, D), 1.0, 6.0, ((0, 32),))
    cache_values = gaussian(arg_keys[3], (CACHE_ROWS, D), 1.0, 6.0, ((0, 32),))
    block_dest_keys = jax.random.split(jax.random.fold_in(arg_keys[4], 1), BLOCKS // CB_DEV)
    block_dest_turns = jax.random.permutation(jax.random.fold_in(arg_keys[4], 3), BLOCKS // CB_DEV)
    block_dest = jax.vmap(lambda own, number: deal_out(jax.random.fold_in(arg_keys[4], 2), own, number, CB_DEV, N_SHARD, 1, MOST, 2))(block_dest_keys, block_dest_turns).reshape((BLOCKS, 1))
    w_in = gaussian(arg_keys[5], (D, 2 * D), D ** -0.5, 0.25)
    w_out = gaussian(arg_keys[6], (D, D), D ** -0.5, 0.25)
    return {"cand_table": cand_table, "inverse": inverse, "cache_keys": cache_keys, "cache_values": cache_values, "block_dest": block_dest, "w_in": w_in, "w_out": w_out}


def layer_norm(inputs):
    center = inputs - lax.optimization_barrier(jnp.mean(inputs, axis=-1, keepdims=True))
    spread = lax.optimization_barrier(jnp.mean(center * center, axis=-1, keepdims=True))
    return center * lax.rsqrt(spread + 1e-05)

def reference(cand_table, inverse, cache_keys, cache_values, block_dest, w_in, w_out):
    head_size = D // H
    score_scale = 1.0 / math.sqrt(head_size)
    device_count = N_GRP * N_SHARD
    embedded = jnp.take(cand_table, inverse, axis=0)
    normed = layer_norm(embedded.astype(jnp.float32)).astype(jnp.bfloat16)
    projected = jax.nn.silu(jnp.dot(normed, w_in, preferred_element_type=jnp.float32))
    gate_u = projected[:, :D].astype(jnp.bfloat16)
    query_low = lax.optimization_barrier(projected[:, D:].astype(jnp.bfloat16))
    queries = query_low.astype(jnp.float32).reshape(device_count, CAND, H, head_size)
    key_blocks = cache_keys.reshape(device_count, CB_DEV, BLK, H, head_size)
    value_blocks = cache_values.reshape(device_count, CB_DEV, BLK, H, head_size)
    scorer_ids = block_dest.reshape(device_count, CB_DEV)
    group_base = jnp.arange(device_count, dtype=jnp.int32) // N_SHARD * N_SHARD

    def owner_step(running, owner):
        targets = group_base[owner] + scorer_ids[owner]
        chosen = queries[targets]
        key_rows = key_blocks[owner].astype(jnp.float32)
        value_rows = value_blocks[owner].astype(jnp.float32)
        scores = jnp.einsum('bchd,bkhd->bhck', chosen, key_rows, precision=lax.Precision.HIGHEST)
        weight_low = lax.optimization_barrier(jax.nn.silu(score_scale * scores).astype(jnp.bfloat16))
        parts = jnp.einsum('bhck,bkhd->bchd', weight_low.astype(jnp.float32), value_rows, precision=lax.Precision.HIGHEST)
        return (running.at[targets].add(parts), None)
    start_sums = jnp.zeros((device_count, CAND, H, head_size), jnp.float32)
    attended, _ = lax.scan(owner_step, start_sums, jnp.arange(device_count, dtype=jnp.int32))
    attended = attended.reshape(device_count * CAND, D)
    gated_rows = (layer_norm(attended) * gate_u.astype(jnp.float32)).astype(jnp.bfloat16)
    return jnp.dot(gated_rows, w_out, preferred_element_type=jnp.float32).astype(jnp.bfloat16)
```

```python
import functools

import jax
import jax.numpy as jnp
from jax import lax
from jax.experimental import pallas as pl
from jax.experimental.pallas import tpu as pltpu
from jax.sharding import PartitionSpec as P

H = 8
BLK = 128
MOST = 2
PAIR = 128


def layer_norm(inputs):
    center = inputs - jnp.mean(inputs, axis=-1, keepdims=True)
    spread = jnp.mean(center * center, axis=-1, keepdims=True)
    return center * lax.rsqrt(spread + 1e-05)


def silu_of_half(half):
    return half + half * jnp.tanh(half)


def project(rows, weights):
    normed = layer_norm(rows.astype(jnp.float32)).astype(jnp.bfloat16)
    product = jnp.dot(normed, weights, preferred_element_type=jnp.float32)
    return silu_of_half(0.5 * product)


def select(index_column, table):
    rows = table.shape[0]
    ids = lax.broadcasted_iota(jnp.int32, (index_column.shape[0], rows), 1)
    one_hot = jnp.where(index_column == ids, 1.0, 0.0).astype(jnp.bfloat16)
    return jnp.dot(one_hot, table, preferred_element_type=jnp.float32).astype(jnp.bfloat16)


def partial_kernel(
    scorers, cand, dest_ref, inverse_ref, table_ref, w_ref, keys_ref, values_ref, out_ref,
    unique_ref, count_ref, slot_ref,
):
    width = table_ref.shape[1]
    head = width // H
    blocks = dest_ref.shape[0]
    chunk = 512

    @pl.loop(0, table_ref.shape[0] // chunk)
    def _(step):
        rows = pl.ds(pl.multiple_of(step * chunk, chunk), chunk)
        queries = project(table_ref[rows, :], w_ref[...]).astype(jnp.bfloat16)
        unique_ref[rows, :] = queries * jnp.bfloat16(0.5 / head**0.5)

    @pl.loop(0, scorers)
    def _(scorer):
        count_ref[scorer] = 0
        for slot in range(MOST):
            slot_ref[scorer * MOST + slot] = 0

    @pl.loop(0, blocks)
    def _(block):
        scorer = dest_ref[block]
        place = count_ref[scorer]
        slot_ref[scorer * MOST + place] = block
        count_ref[scorer] = place + 1

    lane = lax.broadcasted_iota(jnp.int32, (1, PAIR), 1)

    @pl.loop(0, scorers)
    def _(scorer):
        rows = pl.ds(pl.multiple_of(scorer * cand, cand), cand)
        count = count_ref[scorer]

        @pl.when(count == 0)
        def _():
            out_ref[rows, :] = jnp.zeros((cand, width), out_ref.dtype)

        @pl.when(count > 0)
        def _():
            queries = select(inverse_ref[rows, :], unique_ref[...])
            second = jnp.where(count > 1, 1.0, 0.0).astype(jnp.bfloat16)
            first_block, second_block = slot_ref[scorer * MOST], slot_ref[scorer * MOST + 1]
            for pair in range(width // PAIR):
                at = slice(pair * PAIR, (pair + 1) * PAIR)
                keys = jnp.concatenate(
                    [keys_ref[first_block, :, at], keys_ref[second_block, :, at] * second], axis=0
                )
                values = jnp.concatenate(
                    [values_ref[first_block, :, at], values_ref[second_block, :, at]], axis=0
                )
                total = jnp.zeros((cand, PAIR), jnp.float32)
                for inner in range(PAIR // head):
                    own = jnp.where(lane // head == inner, 1.0, 0.0).astype(jnp.bfloat16)
                    half = lax.dot_general(
                        queries[:, at] * own, keys, (((1,), (1,)), ((), ())),
                        preferred_element_type=jnp.float32,
                    )
                    weight = silu_of_half(half).astype(jnp.bfloat16)
                    total += jnp.dot(weight, values * own, preferred_element_type=jnp.float32)
                out_ref[rows, at] = total.astype(out_ref.dtype)


def gate_kernel(inverse_ref, table_ref, w_ref, gate_ref):
    gate_ref[...] = project(select(inverse_ref[...], table_ref[...]), w_ref[...]).astype(gate_ref.dtype)


def final_kernel(attended_ref, gate_ref, w_ref, out_ref):
    gated = layer_norm(attended_ref[...].astype(jnp.float32)) * gate_ref[...].astype(jnp.float32)
    out_ref[...] = jnp.dot(
        gated.astype(jnp.bfloat16), w_ref[...], preferred_element_type=jnp.float32
    ).astype(out_ref.dtype)


VMEM = pl.BlockSpec(memory_space=pltpu.VMEM)
SMEM = pl.BlockSpec(memory_space=pltpu.SMEM)


def on_device(cand_table, inverse, cache_keys, cache_values, block_dest, w_in, w_out):
    width = w_out.shape[0]
    cand = inverse.shape[0]
    scorers = lax.axis_size("shard")
    blocks = block_dest.shape[0]
    table = lax.all_gather(cand_table, "grp", axis=0, tiled=True)
    every_inverse = lax.all_gather(inverse, "shard", axis=0, tiled=True)
    unique = table.shape[0]
    partial = pl.pallas_call(
        functools.partial(partial_kernel, scorers, cand),
        out_shape=jax.ShapeDtypeStruct((scorers * cand, width), jnp.bfloat16),
        in_specs=[SMEM, VMEM, VMEM, VMEM, VMEM, VMEM],
        out_specs=VMEM,
        scratch_shapes=[
            pltpu.VMEM((unique, width), jnp.bfloat16),
            pltpu.SMEM((scorers,), jnp.int32),
            pltpu.SMEM((scorers * MOST,), jnp.int32),
        ],
        compiler_params=pltpu.CompilerParams(vmem_limit_bytes=48 * 2**20),
        name="partial_sums",
    )(
        block_dest[:, 0],
        every_inverse[:, None],
        table,
        w_in[:, width:],
        cache_keys.reshape(blocks, BLK, width),
        cache_values.reshape(blocks, BLK, width),
    )
    attended = lax.psum_scatter(partial, "shard", scatter_dimension=0, tiled=True)
    gate = pl.pallas_call(
        gate_kernel,
        out_shape=jax.ShapeDtypeStruct((cand, width), jnp.bfloat16),
        in_specs=[VMEM] * 3,
        out_specs=VMEM,
        compiler_params=pltpu.CompilerParams(vmem_limit_bytes=32 * 2**20),
        cost_estimate=pl.CostEstimate(
            flops=2 * cand * width * (unique + width), bytes_accessed=2 * unique * width, transcendentals=0
        ),
        name="gate",
    )(inverse[:, None], table, w_in[:, :width])
    return pl.pallas_call(
        final_kernel,
        out_shape=jax.ShapeDtypeStruct((cand, width), jnp.bfloat16),
        in_specs=[VMEM] * 3,
        out_specs=VMEM,
        name="final",
    )(attended, gate, w_out)


def solution(mesh):
    rows = P(("grp", "shard"), None)
    in_specs = (P("grp", None), P(("grp", "shard")), rows, rows, rows, P(), P())
    return jax.shard_map(
        on_device, mesh=mesh, in_specs=in_specs, out_specs=rows, check_vma=False
    )
```

```python
import functools

import jax
import jax.numpy as jnp
from jax import lax
from jax.experimental import pallas as pl
from jax.experimental.pallas import tpu as pltpu
from jax.sharding import PartitionSpec as P

H = 8
BLK = 128
MOST = 2
PAIR = 128


def layer_norm(inputs):
    center = inputs - jnp.mean(inputs, axis=-1, keepdims=True)
    spread = jnp.mean(center * center, axis=-1, keepdims=True)
    return center * lax.rsqrt(spread + 1e-05)


def silu_of_half(half):
    return half + half * jnp.tanh(half)


def project(rows, weights):
    normed = layer_norm(rows.astype(jnp.float32)).astype(jnp.bfloat16)
    product = jnp.dot(normed, weights, preferred_element_type=jnp.float32)
    return silu_of_half(0.5 * product)


def select(index_column, table):
    rows = table.shape[0]
    ids = lax.broadcasted_iota(jnp.int32, (index_column.shape[0], rows), 1)
    one_hot = jnp.where(index_column == ids, 1.0, 0.0).astype(jnp.bfloat16)
    return jnp.dot(one_hot, table, preferred_element_type=jnp.float32).astype(jnp.bfloat16)


def partial_kernel(
    scorers, cand, dest_ref, inverse_ref, table_ref, w_ref, keys_ref, values_ref, out_ref,
    unique_ref, count_ref, slot_ref,
):
    width = table_ref.shape[1]
    head = width // H
    blocks = dest_ref.shape[0]
    chunk = 512

    @pl.loop(0, table_ref.shape[0] // chunk)
    def _(step):
        rows = pl.ds(pl.multiple_of(step * chunk, chunk), chunk)
        queries = project(table_ref[rows, :], w_ref[...]).astype(jnp.bfloat16)
        unique_ref[rows, :] = queries * jnp.bfloat16(0.5 / head**0.5)

    @pl.loop(0, scorers)
    def _(scorer):
        count_ref[scorer] = 0
        for slot in range(MOST):
            slot_ref[scorer * MOST + slot] = 0

    @pl.loop(0, blocks)
    def _(block):
        scorer = dest_ref[block]
        place = count_ref[scorer]
        slot_ref[scorer * MOST + place] = block
        count_ref[scorer] = place + 1

    lane = lax.broadcasted_iota(jnp.int32, (1, PAIR), 1)

    @pl.loop(0, scorers)
    def _(scorer):
        rows = pl.ds(pl.multiple_of(scorer * cand, cand), cand)
        count = count_ref[scorer]

        @pl.when(count == 0)
        def _():
            out_ref[rows, :] = jnp.zeros((cand, width), out_ref.dtype)

        @pl.when(count > 0)
        def _():
            queries = select(inverse_ref[rows, :], unique_ref[...])
            second = jnp.where(count > 1, 1.0, 0.0).astype(jnp.bfloat16)
            first_block, second_block = slot_ref[scorer * MOST], slot_ref[scorer * MOST + 1]
            for pair in range(width // PAIR):
                at = slice(pair * PAIR, (pair + 1) * PAIR)
                keys = jnp.concatenate(
                    [keys_ref[first_block, :, at], keys_ref[second_block, :, at] * second], axis=0
                )
                values = jnp.concatenate(
                    [values_ref[first_block, :, at], values_ref[second_block, :, at]], axis=0
                )
                total = jnp.zeros((cand, PAIR), jnp.float32)
                for inner in range(PAIR // head):
                    own = jnp.where(lane // head == inner, 1.0, 0.0).astype(jnp.bfloat16)
                    half = lax.dot_general(
                        queries[:, at] * own, keys, (((1,), (1,)), ((), ())),
                        preferred_element_type=jnp.float32,
                    )
                    weight = silu_of_half(half).astype(jnp.bfloat16)
                    total += jnp.dot(weight, values * own, preferred_element_type=jnp.float32)
                out_ref[rows, at] = total.astype(out_ref.dtype)


def gate_kernel(inverse_ref, table_ref, w_ref, gate_ref):
    gate_ref[...] = project(select(inverse_ref[...], table_ref[...]), w_ref[...]).astype(gate_ref.dtype)


def send(source, target, send_sem, recv_sem, **device):
    copy = pltpu.make_async_remote_copy(
        src_ref=source, dst_ref=target, send_sem=send_sem, recv_sem=recv_sem,
        device_id=device, device_id_type=pl.DeviceIdType.MESH,
    )
    copy.start()
    return copy


def greet(devices):
    barrier = pltpu.get_barrier_semaphore()
    for device in devices:
        pl.semaphore_signal(
            barrier, inc=1, device_id=device, device_id_type=pl.DeviceIdType.MESH
        )
    pl.semaphore_wait(barrier, len(devices))


def gather_kernel(
    groups, scorers, own_ref, inverse_ref, table_ref, every_ref,
    keep_sem, far_send, far_recv, near_send, near_recv, index_send, index_recv,
):
    group, scorer = lax.axis_index("grp"), lax.axis_index("shard")
    chips = groups // 2
    chip, core = group // 2, group % 2
    other_core = chip * 2 + 1 - core
    far = {k: lax.rem(chip + k, chips) * 2 + core for k in range(1, chips)}
    from_far = {k: lax.rem(chip + chips - k, chips) * 2 + core for k in range(1, chips)}
    peers = {k: lax.rem(scorer + k, scorers) for k in range(1, scorers)}
    greet(
        [{"grp": g} for g in far.values()] + [{"grp": other_core}]
        + [{"shard": s} for s in peers.values()]
    )
    copies = [
        send(own_ref, table_ref.at[group], far_send.at[k], far_recv.at[k], grp=far[k])
        for k in far
    ]
    copies += [
        send(inverse_ref, every_ref.at[scorer], index_send.at[k], index_recv.at[k], shard=peers[k])
        for k in peers
    ]
    relays = [
        send(own_ref, table_ref.at[group], near_send.at[0], near_recv.at[0], grp=other_core)
    ]
    keep = pltpu.make_async_copy(own_ref, table_ref.at[group], keep_sem)
    keep.start()
    every_ref[scorer] = inverse_ref[...]
    for k, copy in zip(far, copies):
        copy.wait_recv()
        block = table_ref.at[from_far[k]]
        relays.append(
            send(block, block, near_send.at[k], near_recv.at[k], grp=other_core)
        )
    keep.wait()
    for copy in copies:
        copy.wait_send()
    for copy in copies[len(far):]:
        copy.wait_recv()
    for copy in relays:
        copy.wait()


def reduce_kernel(
    scorers, cand, partial_ref, gate_ref, w_ref, out_ref, pair_ref, sum_ref, got_ref,
    pair_send, pair_recv, far_send, far_recv,
):
    me = lax.axis_index("shard")
    places = scorers // 2
    place, side = me // 2, me % 2
    partner = place * 2 + 1 - side
    target = {k: lax.rem(place + k, places) for k in range(places)}
    greet([{"shard": partner}] + [{"shard": target[k] * 2 + side} for k in range(1, places)])

    def rows(scorer):
        return pl.ds(pl.multiple_of(scorer * cand, cand), cand)

    order = [*range(places // 2, places), *range(1, places // 2), 0]
    pairs = {
        k: send(
            partial_ref.at[rows(target[k] * 2 + 1 - side)], pair_ref.at[k],
            pair_send.at[k], pair_recv.at[k], shard=partner,
        )
        for k in order
    }
    far = []
    for k in order:
        pairs[k].wait_recv()
        total = partial_ref[rows(target[k] * 2 + side), :].astype(jnp.float32) + pair_ref[k].astype(
            jnp.float32
        )
        if k:
            sum_ref[k] = total.astype(sum_ref.dtype)
            far.append(
                send(
                    sum_ref.at[k], got_ref.at[k], far_send.at[k], far_recv.at[k],
                    shard=target[k] * 2 + side,
                )
            )
    for k, copy in zip(order, far):
        copy.wait_recv()
        total += got_ref[k].astype(jnp.float32)
    gated = layer_norm(total) * gate_ref[...].astype(jnp.float32)
    out_ref[...] = jnp.dot(
        gated.astype(jnp.bfloat16), w_ref[...], preferred_element_type=jnp.float32
    ).astype(out_ref.dtype)
    for k in order:
        pairs[k].wait_send()
    for copy in far:
        copy.wait_send()


VMEM = pl.BlockSpec(memory_space=pltpu.VMEM)
SMEM = pl.BlockSpec(memory_space=pltpu.SMEM)


def on_device(cand_table, inverse, cache_keys, cache_values, block_dest, w_in, w_out):
    width = w_out.shape[0]
    cand = inverse.shape[0]
    scorers = lax.axis_size("shard")
    blocks = block_dest.shape[0]
    groups = lax.axis_size("grp")
    dma = pltpu.SemaphoreType.DMA
    table, every_inverse = pl.pallas_call(
        functools.partial(gather_kernel, groups, scorers),
        out_shape=(
            jax.ShapeDtypeStruct((groups, *cand_table.shape), cand_table.dtype),
            jax.ShapeDtypeStruct((scorers, 1, cand), inverse.dtype),
        ),
        in_specs=[VMEM] * 2,
        out_specs=(VMEM, VMEM),
        scratch_shapes=[
            dma, dma((groups // 2,)), dma((groups // 2,)), dma((groups // 2,)), dma((groups // 2,)),
            dma((scorers,)), dma((scorers,)),
        ],
        compiler_params=pltpu.CompilerParams(
            collective_id=0, has_side_effects=True, vmem_limit_bytes=24 * 2**20
        ),
        name="gather",
    )(cand_table, inverse[None, :])
    table = table.reshape(-1, width)
    every_inverse = every_inverse.reshape(-1)
    unique = table.shape[0]
    partial = pl.pallas_call(
        functools.partial(partial_kernel, scorers, cand),
        out_shape=jax.ShapeDtypeStruct((scorers * cand, width), jnp.bfloat16),
        in_specs=[SMEM, VMEM, VMEM, VMEM, VMEM, VMEM],
        out_specs=VMEM,
        scratch_shapes=[
            pltpu.VMEM((unique, width), jnp.bfloat16),
            pltpu.SMEM((scorers,), jnp.int32),
            pltpu.SMEM((scorers * MOST,), jnp.int32),
        ],
        compiler_params=pltpu.CompilerParams(vmem_limit_bytes=48 * 2**20),
        name="partial_sums",
    )(
        block_dest[:, 0],
        every_inverse[:, None],
        table,
        w_in[:, width:],
        cache_keys.reshape(blocks, BLK, width),
        cache_values.reshape(blocks, BLK, width),
    )
    gate = pl.pallas_call(
        gate_kernel,
        out_shape=jax.ShapeDtypeStruct((cand, width), jnp.bfloat16),
        in_specs=[VMEM] * 3,
        out_specs=VMEM,
        compiler_params=pltpu.CompilerParams(vmem_limit_bytes=32 * 2**20),
        cost_estimate=pl.CostEstimate(
            flops=2 * cand * width * (unique + width), bytes_accessed=2 * unique * width, transcendentals=0
        ),
        name="gate",
    )(inverse[:, None], table, w_in[:, :width])
    places = scorers // 2
    return pl.pallas_call(
        functools.partial(reduce_kernel, scorers, cand),
        out_shape=jax.ShapeDtypeStruct((cand, width), jnp.bfloat16),
        in_specs=[VMEM] * 3,
        out_specs=VMEM,
        scratch_shapes=[pltpu.VMEM((places, cand, width), jnp.bfloat16)] * 3 + [dma((places,))] * 4,
        compiler_params=pltpu.CompilerParams(
            collective_id=1, has_side_effects=True, vmem_limit_bytes=40 * 2**20
        ),
        name="reduce",
    )(partial, gate, w_out)


def solution(mesh):
    rows = P(("grp", "shard"), None)
    in_specs = (P("grp", None), P(("grp", "shard")), rows, rows, rows, P(), P())
    return jax.shard_map(
        on_device, mesh=mesh, in_specs=in_specs, out_specs=rows, check_vma=False
    )
```

```python
import functools

import jax
import jax.numpy as jnp
from jax import lax
from jax.experimental import pallas as pl
from jax.experimental.pallas import tpu as pltpu
from jax.sharding import PartitionSpec as P

H = 8
BLK = 128
MOST = 2
PAIR = 128


def layer_norm(inputs):
    center = inputs - jnp.mean(inputs, axis=-1, keepdims=True)
    spread = jnp.mean(center * center, axis=-1, keepdims=True)
    return center * lax.rsqrt(spread + 1e-05)


def silu_of_half(half):
    return half + half * jnp.tanh(half)


def project(rows, weights):
    normed = layer_norm(rows.astype(jnp.float32)).astype(jnp.bfloat16)
    product = jnp.dot(normed, weights, preferred_element_type=jnp.float32)
    return silu_of_half(0.5 * product)


def select(index_column, table):
    rows = table.shape[0]
    ids = lax.broadcasted_iota(jnp.int32, (index_column.shape[0], rows), 1)
    one_hot = jnp.where(index_column == ids, 1.0, 0.0).astype(jnp.bfloat16)
    return jnp.dot(one_hot, table, preferred_element_type=jnp.float32).astype(jnp.bfloat16)


def arrange_kernel(scorers, dest_ref, keys_ref, values_ref, out_keys_ref, out_values_ref, count_ref, sems):
    @pl.loop(0, scorers)
    def _(scorer):
        count_ref[scorer] = 0

    @pl.loop(0, dest_ref.shape[0])
    def _(block):
        scorer = dest_ref[block]
        place = count_ref[scorer]
        rows = pl.ds(pl.multiple_of(place * BLK, BLK), BLK)
        count_ref[scorer] = place + 1
        pltpu.make_async_copy(keys_ref.at[block], out_keys_ref.at[scorer, rows], sems.at[0, block]).start()
        pltpu.make_async_copy(values_ref.at[block], out_values_ref.at[scorer, rows], sems.at[1, block]).start()

    @pl.loop(0, scorers)
    def _(scorer):
        for place in range(MOST):
            @pl.when(count_ref[scorer] <= place)
            def _():
                rows = pl.ds(place * BLK, BLK)
                empty = jnp.zeros((BLK, keys_ref.shape[2]), out_keys_ref.dtype)
                out_keys_ref[scorer, rows, :] = empty
                out_values_ref[scorer, rows, :] = empty

    @pl.loop(0, dest_ref.shape[0])
    def _(block):
        rows = pl.ds(0, BLK)
        pltpu.make_async_copy(keys_ref.at[block], out_keys_ref.at[0, rows], sems.at[0, block]).wait()
        pltpu.make_async_copy(values_ref.at[block], out_values_ref.at[0, rows], sems.at[1, block]).wait()


def attend(queries, keys_ref, values_ref, scorer, out_ref, rows):
    width = queries.shape[1]
    head = width // H
    lane = lax.broadcasted_iota(jnp.int32, (1, PAIR), 1)
    for pair in range(width // PAIR):
        at = slice(pair * PAIR, (pair + 1) * PAIR)
        keys, values = keys_ref[scorer, :, at], values_ref[scorer, :, at]
        total = jnp.zeros((queries.shape[0], PAIR), jnp.float32)
        for inner in range(PAIR // head):
            own = jnp.where(lane // head == inner, 1.0, 0.0).astype(jnp.bfloat16)
            half = lax.dot_general(
                queries[:, at] * own, keys, (((1,), (1,)), ((), ())),
                preferred_element_type=jnp.float32,
            )
            weight = silu_of_half(half).astype(jnp.bfloat16)
            total += jnp.dot(weight, values * own, preferred_element_type=jnp.float32)
        out_ref[rows, at] = total.astype(out_ref.dtype)


def send(source, target, send_sem, recv_sem, **device):
    copy = pltpu.make_async_remote_copy(
        src_ref=source, dst_ref=target, send_sem=send_sem, recv_sem=recv_sem,
        device_id=device, device_id_type=pl.DeviceIdType.MESH,
    )
    copy.start()
    return copy


def greet(devices):
    barrier = pltpu.get_barrier_semaphore()
    for device in devices:
        pl.semaphore_signal(
            barrier, inc=1, device_id=device, device_id_type=pl.DeviceIdType.MESH
        )
    pl.semaphore_wait(barrier, len(devices))


def gather_kernel(
    groups, scorers, own_ref, inverse_ref, w_ref, table_ref, every_ref, unique_ref,
    keep_sem, far_send, far_recv, near_send, near_recv, index_send, index_recv,
):
    group, scorer = lax.axis_index("grp"), lax.axis_index("shard")
    chips = groups // 2
    chip, core = group // 2, group % 2
    other_core = chip * 2 + 1 - core
    far = {k: lax.rem(chip + k, chips) * 2 + core for k in range(1, chips)}
    from_far = {k: lax.rem(chip + chips - k, chips) * 2 + core for k in range(1, chips)}
    peers = {k: lax.rem(scorer + k, scorers) for k in range(1, scorers)}
    greet(
        [{"grp": g} for g in far.values()] + [{"grp": other_core}]
        + [{"shard": s} for s in peers.values()]
    )
    copies = [
        send(own_ref, table_ref.at[group], far_send.at[k], far_recv.at[k], grp=far[k])
        for k in far
    ]
    copies += [
        send(inverse_ref, every_ref.at[scorer], index_send.at[k], index_recv.at[k], shard=peers[k])
        for k in peers
    ]
    relays = [
        send(own_ref, table_ref.at[group], near_send.at[0], near_recv.at[0], grp=other_core)
    ]
    keep = pltpu.make_async_copy(own_ref, table_ref.at[group], keep_sem)
    keep.start()
    every_ref[scorer] = inverse_ref[...]

    def project_rows(block, rows):
        width = w_ref.shape[0]
        queries = project(rows, w_ref[:, width:]).astype(jnp.bfloat16)
        unique_ref[block] = queries * jnp.bfloat16(0.5 / (width // H) ** 0.5)

    project_rows(group, own_ref[...])
    relays[0].wait_recv()
    project_rows(other_core, table_ref[other_core])
    for k, copy in zip(far, copies):
        copy.wait_recv()
        block = table_ref.at[from_far[k]]
        relays.append(
            send(block, block, near_send.at[k], near_recv.at[k], grp=other_core)
        )
        project_rows(from_far[k], table_ref[from_far[k]])
        relays[k].wait_recv()
        twin = from_far[k] + 1 - 2 * core
        project_rows(twin, table_ref[twin])
    keep.wait()
    for copy in copies:
        copy.wait_send()
    for copy in copies[len(far):]:
        copy.wait_recv()
    for copy in relays:
        copy.wait_send()


def reduce_kernel(
    scorers, cand, inverse_ref, unique_ref, keys_ref, values_ref, table_ref, w_in_ref, w_out_ref, out_ref,
    partial_ref, pair_ref, sum_ref, got_ref, pair_send, pair_recv, far_send, far_recv,
):
    me = lax.axis_index("shard")
    width = w_out_ref.shape[0]
    places = scorers // 2
    place, side = me // 2, me % 2
    partner = place * 2 + 1 - side
    greet(
        [{"shard": partner}]
        + [{"shard": lax.rem(place + k, places) * 2 + side} for k in range(1, places)]
    )

    def rows(scorer):
        return pl.ds(pl.multiple_of(scorer * cand, cand), cand)

    def pair_copy(k):
        scorer = lax.rem(place + k, places) * 2 + 1 - side
        return pltpu.make_async_remote_copy(
            src_ref=partial_ref.at[rows(scorer)], dst_ref=pair_ref.at[k],
            send_sem=pair_send.at[k], recv_sem=pair_recv.at[k],
            device_id={"shard": partner}, device_id_type=pl.DeviceIdType.MESH,
        )

    def far_copy(k):
        return pltpu.make_async_remote_copy(
            src_ref=sum_ref.at[k], dst_ref=got_ref.at[k],
            send_sem=far_send.at[k], recv_sem=far_recv.at[k],
            device_id={"shard": lax.rem(place + k, places) * 2 + side},
            device_id_type=pl.DeviceIdType.MESH,
        )

    def fill(scorer):
        queries = select(inverse_ref[rows(scorer), :], unique_ref[...])
        attend(queries, keys_ref, values_ref, scorer, partial_ref, rows(scorer))

    def pair_sum(k):
        pair_copy(k).wait_recv()
        own = partial_ref[rows(lax.rem(place + k, places) * 2 + side), :]
        return own.astype(jnp.float32) + pair_ref[k].astype(jnp.float32)

    @pl.loop(0, places)
    def _(step):
        k = lax.rem(step + 1, places)
        pair = lax.rem(place + k, places) * 2
        fill(pair + 1 - side)
        pair_copy(k).start()
        fill(pair + side)

        @pl.when(step > 0)
        def _():
            sum_ref[step] = pair_sum(step).astype(sum_ref.dtype)
            far_copy(step).start()

    embedded = select(inverse_ref[rows(me), :], table_ref[...])
    gate = project(embedded, w_in_ref[:, :width]).astype(jnp.bfloat16)
    total = pair_sum(0)
    for k in range(1, places):
        far_copy(k).wait_recv()
        total += got_ref[k].astype(jnp.float32)
    gated = layer_norm(total) * gate.astype(jnp.float32)
    out_ref[...] = jnp.dot(
        gated.astype(jnp.bfloat16), w_out_ref[...], preferred_element_type=jnp.float32
    ).astype(out_ref.dtype)

    for k in range(places):
        pair_copy(k).wait_send()
        if k:
            far_copy(k).wait_send()


VMEM = pl.BlockSpec(memory_space=pltpu.VMEM)
SMEM = pl.BlockSpec(memory_space=pltpu.SMEM)


def on_device(cand_table, inverse, cache_keys, cache_values, block_dest, w_in, w_out):
    width = w_out.shape[0]
    cand = inverse.shape[0]
    scorers = lax.axis_size("shard")
    blocks = block_dest.shape[0]
    groups = lax.axis_size("grp")
    dma = pltpu.SemaphoreType.DMA
    table, every_inverse, unique = pl.pallas_call(
        functools.partial(gather_kernel, groups, scorers),
        out_shape=(
            jax.ShapeDtypeStruct((groups, *cand_table.shape), cand_table.dtype),
            jax.ShapeDtypeStruct((scorers, 1, cand), inverse.dtype),
            jax.ShapeDtypeStruct((groups, *cand_table.shape), cand_table.dtype),
        ),
        in_specs=[VMEM] * 3,
        out_specs=(VMEM, VMEM, VMEM),
        scratch_shapes=[
            dma, dma((groups // 2,)), dma((groups // 2,)), dma((groups // 2,)), dma((groups // 2,)),
            dma((scorers,)), dma((scorers,)),
        ],
        compiler_params=pltpu.CompilerParams(
            collective_id=0, has_side_effects=True, vmem_limit_bytes=24 * 2**20
        ),
        name="gather",
    )(cand_table, inverse[None, :], w_in)
    ordered = jax.ShapeDtypeStruct((scorers, MOST * BLK, width), cache_keys.dtype)
    keys, values = pl.pallas_call(
        functools.partial(arrange_kernel, scorers),
        out_shape=(ordered, ordered),
        in_specs=[SMEM, pl.BlockSpec(memory_space=pl.ANY), pl.BlockSpec(memory_space=pl.ANY)],
        out_specs=(VMEM, VMEM),
        scratch_shapes=[pltpu.SMEM((scorers,), jnp.int32), dma((2, blocks))],
        compiler_params=pltpu.CompilerParams(vmem_limit_bytes=24 * 2**20),
        name="arrange",
    )(
        block_dest[:, 0],
        cache_keys.reshape(blocks, BLK, width),
        cache_values.reshape(blocks, BLK, width),
    )
    places = scorers // 2
    buffers = pltpu.VMEM((places, cand, width), jnp.bfloat16)
    return pl.pallas_call(
        functools.partial(reduce_kernel, scorers, cand),
        out_shape=jax.ShapeDtypeStruct((cand, width), jnp.bfloat16),
        in_specs=[VMEM] * 7,
        out_specs=VMEM,
        scratch_shapes=[pltpu.VMEM((scorers * cand, width), jnp.bfloat16)]
        + [buffers] * 3
        + [dma((places,))] * 4,
        compiler_params=pltpu.CompilerParams(
            collective_id=1, has_side_effects=True, vmem_limit_bytes=58 * 2**20
        ),
        name="attend_and_reduce",
    )(
        every_inverse.reshape(-1)[:, None], unique.reshape(-1, width), keys, values,
        table.reshape(-1, width), w_in, w_out,
    )


def solution(mesh):
    rows = P(("grp", "shard"), None)
    in_specs = (P("grp", None), P(("grp", "shard")), rows, rows, rows, P(), P())
    return jax.shard_map(
        on_device, mesh=mesh, in_specs=in_specs, out_specs=rows, check_vma=False
    )
```

```python
import functools

import jax
import jax.numpy as jnp
from jax import lax
from jax.experimental import pallas as pl
from jax.experimental.pallas import tpu as pltpu
from jax.sharding import PartitionSpec as P

H = 8
BLK = 128
MOST = 2
PAIR = 128


def layer_norm(inputs):
    center = inputs - jnp.mean(inputs, axis=-1, keepdims=True)
    spread = jnp.mean(center * center, axis=-1, keepdims=True)
    return center * lax.rsqrt(spread + 1e-05)


def silu_of_half(half):
    return half + half * jnp.tanh(half)


def project(rows, weights):
    normed = layer_norm(rows.astype(jnp.float32)).astype(jnp.bfloat16)
    product = jnp.dot(normed, weights, preferred_element_type=jnp.float32)
    return silu_of_half(0.5 * product)


def select(index_column, table):
    rows = table.shape[0]
    ids = lax.broadcasted_iota(jnp.int32, (index_column.shape[0], rows), 1)
    one_hot = jnp.where(index_column == ids, 1.0, 0.0).astype(jnp.bfloat16)
    return jnp.dot(one_hot, table, preferred_element_type=jnp.float32).astype(jnp.bfloat16)


def arrange_kernel(scorers, dest_ref, keys_ref, values_ref, out_keys_ref, out_values_ref, count_ref, sems):
    @pl.loop(0, scorers)
    def _(scorer):
        count_ref[scorer] = 0

    @pl.loop(0, dest_ref.shape[0])
    def _(block):
        scorer = dest_ref[block]
        place = count_ref[scorer]
        rows = pl.ds(pl.multiple_of(place * BLK, BLK), BLK)
        count_ref[scorer] = place + 1
        pltpu.make_async_copy(keys_ref.at[block], out_keys_ref.at[scorer, rows], sems.at[0, block]).start()
        pltpu.make_async_copy(values_ref.at[block], out_values_ref.at[scorer, rows], sems.at[1, block]).start()

    @pl.loop(0, scorers)
    def _(scorer):
        for place in range(MOST):
            @pl.when(count_ref[scorer] <= place)
            def _():
                rows = pl.ds(place * BLK, BLK)
                empty = jnp.zeros((BLK, keys_ref.shape[2]), out_keys_ref.dtype)
                out_keys_ref[scorer, rows, :] = empty
                out_values_ref[scorer, rows, :] = empty

    @pl.loop(0, dest_ref.shape[0])
    def _(block):
        rows = pl.ds(0, BLK)
        pltpu.make_async_copy(keys_ref.at[block], out_keys_ref.at[0, rows], sems.at[0, block]).wait()
        pltpu.make_async_copy(values_ref.at[block], out_values_ref.at[0, rows], sems.at[1, block]).wait()


def attend(queries, keys_ref, values_ref, scorer, out_ref, rows):
    width = queries.shape[1]
    head = width // H
    lane = lax.broadcasted_iota(jnp.int32, (1, PAIR), 1)
    for pair in range(width // PAIR):
        at = slice(pair * PAIR, (pair + 1) * PAIR)
        keys, values = keys_ref[scorer, :, at], values_ref[scorer, :, at]
        total = jnp.zeros((queries.shape[0], PAIR), jnp.float32)
        for inner in range(PAIR // head):
            own = jnp.where(lane // head == inner, 1.0, 0.0).astype(jnp.bfloat16)
            half = lax.dot_general(
                queries[:, at] * own, keys, (((1,), (1,)), ((), ())),
                preferred_element_type=jnp.float32,
            )
            weight = silu_of_half(half).astype(jnp.bfloat16)
            total += jnp.dot(weight, values * own, preferred_element_type=jnp.float32)
        out_ref[rows, at] = total.astype(out_ref.dtype)


def send(source, target, send_sem, recv_sem, **device):
    copy = pltpu.make_async_remote_copy(
        src_ref=source, dst_ref=target, send_sem=send_sem, recv_sem=recv_sem,
        device_id=device, device_id_type=pl.DeviceIdType.MESH,
    )
    copy.start()
    return copy


def greet(devices):
    barrier = pltpu.get_barrier_semaphore()
    for device in devices:
        pl.semaphore_signal(
            barrier, inc=1, device_id=device, device_id_type=pl.DeviceIdType.MESH
        )
    pl.semaphore_wait(barrier, len(devices))


def gather_kernel(
    groups, scorers, own_ref, inverse_ref, w_ref, table_ref, every_ref, unique_ref,
    keep_sem, far_send, far_recv, near_send, near_recv, index_send, index_recv,
):
    group, scorer = lax.axis_index("grp"), lax.axis_index("shard")
    chips = groups // 2
    chip, core = group // 2, group % 2
    other_core = chip * 2 + 1 - core
    far = {k: lax.rem(chip + k, chips) * 2 + core for k in range(1, chips)}
    from_far = {k: lax.rem(chip + chips - k, chips) * 2 + core for k in range(1, chips)}
    peers = {k: lax.rem(scorer + k, scorers) for k in range(1, scorers)}
    greet(
        [{"grp": g} for g in far.values()] + [{"grp": other_core}]
        + [{"shard": s} for s in peers.values()]
    )
    copies = [
        send(own_ref, table_ref.at[group], far_send.at[k], far_recv.at[k], grp=far[k])
        for k in far
    ]
    copies += [
        send(inverse_ref, every_ref.at[scorer], index_send.at[k], index_recv.at[k], shard=peers[k])
        for k in peers
    ]
    relays = [
        send(own_ref, table_ref.at[group], near_send.at[0], near_recv.at[0], grp=other_core)
    ]
    keep = pltpu.make_async_copy(own_ref, table_ref.at[group], keep_sem)
    keep.start()
    every_ref[scorer] = inverse_ref[...]

    def project_rows(block, rows):
        width = w_ref.shape[0]
        queries = project(rows, w_ref[:, width:]).astype(jnp.bfloat16)
        unique_ref[block] = queries * jnp.bfloat16(0.5 / (width // H) ** 0.5)

    project_rows(group, own_ref[...])
    relays[0].wait_recv()
    project_rows(other_core, table_ref[other_core])
    for k, copy in zip(far, copies):
        copy.wait_recv()
        block = table_ref.at[from_far[k]]
        relays.append(
            send(block, block, near_send.at[k], near_recv.at[k], grp=other_core)
        )
        project_rows(from_far[k], table_ref[from_far[k]])
        relays[k].wait_recv()
        twin = from_far[k] + 1 - 2 * core
        project_rows(twin, table_ref[twin])
    keep.wait()
    for copy in copies:
        copy.wait_send()
    for copy in copies[len(far):]:
        copy.wait_recv()
    for copy in relays:
        copy.wait_send()


def reduce_kernel(
    scorers, cand, inverse_ref, unique_ref, keys_ref, values_ref, table_ref, w_in_ref, w_out_ref, out_ref,
    partial_ref, pair_ref, sum_ref, got_ref, pair_send, pair_recv, far_send, far_recv,
):
    me = lax.axis_index("shard")
    width = w_out_ref.shape[0]
    places = scorers // 2
    place, side = me // 2, me % 2
    partner = place * 2 + 1 - side
    greet(
        [{"shard": partner}]
        + [{"shard": lax.rem(place + k, places) * 2 + side} for k in range(1, places)]
    )

    def rows(scorer):
        return pl.ds(pl.multiple_of(scorer * cand, cand), cand)

    def pair_copy(k):
        scorer = lax.rem(place + k, places) * 2 + 1 - side
        return pltpu.make_async_remote_copy(
            src_ref=partial_ref.at[rows(scorer)], dst_ref=pair_ref.at[k],
            send_sem=pair_send.at[k], recv_sem=pair_recv.at[k],
            device_id={"shard": partner}, device_id_type=pl.DeviceIdType.MESH,
        )

    def far_copy(k):
        return pltpu.make_async_remote_copy(
            src_ref=sum_ref.at[k], dst_ref=got_ref.at[k],
            send_sem=far_send.at[k], recv_sem=far_recv.at[k],
            device_id={"shard": lax.rem(place + k, places) * 2 + side},
            device_id_type=pl.DeviceIdType.MESH,
        )

    def fill(scorer):
        queries = select(inverse_ref[rows(scorer), :], unique_ref[...])
        attend(queries, keys_ref, values_ref, scorer, partial_ref, rows(scorer))

    def pair_sum(k):
        pair_copy(k).wait_recv()
        own = partial_ref[rows(lax.rem(place + k, places) * 2 + side), :]
        return own.astype(jnp.float32) + pair_ref[k].astype(jnp.float32)

    @pl.loop(0, places)
    def _(step):
        k = lax.rem(step + 1, places)
        pair = lax.rem(place + k, places) * 2
        fill(pair + 1 - side)
        pair_copy(k).start()
        fill(pair + side)

        @pl.when(step > 0)
        def _():
            sum_ref[step] = pair_sum(step).astype(sum_ref.dtype)
            far_copy(step).start()

    embedded = select(inverse_ref[rows(me), :], table_ref[...])
    gate = project(embedded, w_in_ref[:, :width]).astype(jnp.bfloat16)
    total = pair_sum(0)
    for k in range(1, places):
        far_copy(k).wait_recv()
        total += got_ref[k].astype(jnp.float32)
    gated = layer_norm(total) * gate.astype(jnp.float32)
    out_ref[...] = jnp.dot(
        gated.astype(jnp.bfloat16), w_out_ref[...], preferred_element_type=jnp.float32
    ).astype(out_ref.dtype)

    for k in range(places):
        pair_copy(k).wait_send()
        if k:
            far_copy(k).wait_send()


VMEM = pl.BlockSpec(memory_space=pltpu.VMEM)
SMEM = pl.BlockSpec(memory_space=pltpu.SMEM)


def on_device(cand_table, inverse, cache_keys, cache_values, block_dest, w_in, w_out):
    width = w_out.shape[0]
    cand = inverse.shape[0]
    scorers = lax.axis_size("shard")
    blocks = block_dest.shape[0]
    groups = lax.axis_size("grp")
    dma = pltpu.SemaphoreType.DMA
    table, every_inverse, unique = pl.pallas_call(
        functools.partial(gather_kernel, groups, scorers),
        out_shape=(
            jax.ShapeDtypeStruct((groups, *cand_table.shape), cand_table.dtype),
            jax.ShapeDtypeStruct((scorers, 1, cand), inverse.dtype),
            jax.ShapeDtypeStruct((groups, *cand_table.shape), cand_table.dtype),
        ),
        in_specs=[VMEM] * 3,
        out_specs=(VMEM, VMEM, VMEM),
        scratch_shapes=[
            dma, dma((groups // 2,)), dma((groups // 2,)), dma((groups // 2,)), dma((groups // 2,)),
            dma((scorers,)), dma((scorers,)),
        ],
        compiler_params=pltpu.CompilerParams(
            collective_id=0, has_side_effects=True, vmem_limit_bytes=24 * 2**20
        ),
        name="gather",
    )(cand_table, inverse[None, :], w_in)
    ordered = jax.ShapeDtypeStruct((scorers, MOST * BLK, width), cache_keys.dtype)
    keys, values = pl.pallas_call(
        functools.partial(arrange_kernel, scorers),
        out_shape=(ordered, ordered),
        in_specs=[SMEM, pl.BlockSpec(memory_space=pl.ANY), pl.BlockSpec(memory_space=pl.ANY)],
        out_specs=(VMEM, VMEM),
        scratch_shapes=[pltpu.SMEM((scorers,), jnp.int32), dma((2, blocks))],
        compiler_params=pltpu.CompilerParams(vmem_limit_bytes=60 * 2**20),
        name="arrange",
    )(
        block_dest[:, 0],
        cache_keys.reshape(blocks, BLK, width),
        cache_values.reshape(blocks, BLK, width),
    )
    places = scorers // 2
    buffers = pltpu.VMEM((places, cand, width), jnp.bfloat16)
    return pl.pallas_call(
        functools.partial(reduce_kernel, scorers, cand),
        out_shape=jax.ShapeDtypeStruct((cand, width), jnp.bfloat16),
        in_specs=[VMEM] * 7,
        out_specs=VMEM,
        scratch_shapes=[pltpu.VMEM((scorers * cand, width), jnp.bfloat16)]
        + [buffers] * 3
        + [dma((places,))] * 4,
        compiler_params=pltpu.CompilerParams(
            collective_id=1, has_side_effects=True, vmem_limit_bytes=58 * 2**20
        ),
        name="attend_and_reduce",
    )(
        every_inverse.reshape(-1)[:, None], unique.reshape(-1, width), keys, values,
        table.reshape(-1, width), w_in, w_out,
    )


def solution(mesh):
    rows = P(("grp", "shard"), None)
    in_specs = (P("grp", None), P(("grp", "shard")), rows, rows, rows, P(), P())
    return jax.shard_map(
        on_device, mesh=mesh, in_specs=in_specs, out_specs=rows, check_vma=False
    )
```
